512 devices in a mesh: chan: 8 (over x, z_hi), tile: 64 (over y, z_lo, core).
Axes of the slice: x: 4, y: 8, z: 8 (z_hi: 2, z_lo: 4; z = z_hi * 4 + z_lo), core: 2. Of those that a mesh axis runs over, the one named last changes fastest.
Arguments:
- latent: bfloat16 [2, 256, 512, 128], P(None, 'tile', 'chan'), may hold values from -6 to 6
- kernel: bfloat16 [3, 3, 3, 512, 2048], P(None, None, None, 'chan', 'tile'), may hold values from -0.0546875 to 0.0546875
- bias: float32 [2048], replicated, may hold values from -3 to 3
Outputs:
- upsampled: bfloat16 [2, 512, 512, 256], P(None, ('tile', 'chan'))
The draws below stay inside these ranges and needn't reach their ends.
All inputs are finite; a program needn't handle non-finite values.
Results may differ from the reference program's by a relative error of at most 0.015.
Values may be sent and summed in bfloat16 or wider, within the bound.
No kernel may reach another device: no remote copies, remote signals or barrier semaphores. Data moves between devices by JAX's collectives and lax.ppermute only.
A program may use at most 128 MiB of HBM per device.

```python
import jax
import jax.numpy as jnp
from jax import lax

CIN = 512
COUT = 2048
FRAMES = 2
COLS = 128
ROWS = 256
N_CHAN = 8


def level_of(rng, shape, shards, smallest, top_value):
    loudness = 1.0
    for axis_at, blocks in shards:
        steps = jax.random.uniform(jax.random.fold_in(jax.random.fold_in(rng, 6), axis_at), (blocks,), jnp.float32, smallest / len(shards), top_value / len(shards))
        loudness = loudness * jnp.repeat(jnp.exp(steps), shape[axis_at] // blocks).reshape((-1,) + (1,) * (len(shape) - 1 - axis_at))
    return loudness


def centred(key, shape, spread, bound, cuts=(), held_as=jnp.bfloat16):
    result = jax.random.normal(key, shape, jnp.float32) * spread
    if len(cuts) > 0:
        result = level_of(key, shape, cuts, -0.22, 0.18) * result
    return jnp.clip(result, min=-bound, max=bound).astype(held_as)


def setup_inputs(seed: int = 0) -> dict:
    seeds = jax.random.split(jax.random.key(seed), 4)
    return {
        "latent": centred(seeds[0], (FRAMES, ROWS, CIN, COLS), 1.0, 6.0, ((1, 64), (2, 8))),
        "kernel": centred(seeds[1], (3, 3, 3, CIN, COUT), (27 * CIN) ** -0.5, 0.0546875, ((3, 8), (4, 64))),
        "bias": centred(seeds[2], (COUT,), 0.5, 3.0, (), jnp.float32),
    }


def extend(latent):
    first = latent[:1]
    timed = jnp.concatenate([first, first, latent], axis=0)
    return jnp.pad(timed, ((0, 0), (1, 1), (0, 0), (1, 1)))


def conv_taps(extended, kernel, frames, rows, cols):
    windows = []
    for tap_t in range(3):
        for tap_h in range(3):
            for tap_w in range(3):
                windows.append(extended[tap_t:tap_t + frames, tap_h:tap_h + rows, :, tap_w:tap_w + cols])
    stacked = jnp.concatenate(windows, axis=2)
    flat_kernel = kernel.reshape(-1, kernel.shape[-1])
    return jnp.einsum("thkw,ko->thow", stacked.astype(jnp.float32), flat_kernel.astype(jnp.float32))


def shuffle(conv):
    frames, rows, chans, cols = conv.shape
    split = conv.reshape(frames, rows, chans // 4, 2, 2, cols)
    moved = jnp.transpose(split, (0, 1, 3, 2, 5, 4))
    return moved.reshape(frames, rows * 2, chans // 4, cols * 2)


def reference(latent, kernel, bias):
    extended = extend(latent)
    group = CIN // N_CHAN
    total = jnp.zeros((FRAMES, ROWS, COUT, COLS), jnp.float32)
    for index in range(N_CHAN):
        part = conv_taps(extended[:, :, index * group:(index + 1) * group, :], kernel[:, :, :, index * group:(index + 1) * group, :], FRAMES, ROWS, COLS)
        total = total + lax.optimization_barrier(part.astype(jnp.bfloat16)).astype(jnp.float32)
    conv = (total + bias[None, None, :, None]).astype(jnp.bfloat16)
    return shuffle(conv)
```

```python
import functools

import jax
import jax.numpy as jnp
from jax import lax
from jax.experimental import pallas as pl
from jax.experimental.pallas import tpu as pltpu
from jax.sharding import Mesh, PartitionSpec as P

AXES = ("x", "zh", "y", "zl", "k")
SIZES = (4, 2, 8, 4, 2)
NX, NH, NY, NL, NK = SIZES


def ring(size, step):
    return [(i, (i + step) % size) for i in range(size)]


def spread_kernel(kernel):
    k01 = (kernel[0].astype(jnp.float32) + kernel[1].astype(jnp.float32)).astype(kernel.dtype)
    both = jnp.stack([k01, kernel[2]])
    split = both.reshape(2, 3, 3, 64, NX, 2, 2, 2)
    moved = jnp.transpose(split, (4, 6, 1, 2, 7, 5, 0, 3))
    flat = moved.reshape(NX, NH, 1, 3, 3, 2, 2, 128)
    return jnp.broadcast_to(flat, (NX, NH, NL, 3, 3, 2, 2, 128))


def own_chunk(kernel):
    pieces = spread_kernel(kernel).reshape(NX * NH * NL, 3, 3, 2, 2, 128)
    got = lax.all_to_all(pieces, ("x", "zh", "zl"), 0, 0, tiled=True)
    got = got.reshape(NX * NH, NL, 3, 3, 2, 2, 128)
    return jnp.transpose(got, (2, 3, 4, 1, 5, 0, 6)).reshape(3, 3, 16, 1024)


def own_rows(latent):
    core = lax.axis_index("k")
    rows = jnp.transpose(latent, (1, 0, 2, 3))
    edge = jnp.where(core == 0, rows[:1], rows[3:])
    pairs = [(2 * i + 1, 2 * i + 2) for i in range(31)]
    halo = lax.ppermute(edge, ("y", "zl", "k"), pairs + [(b, a) for a, b in pairs])
    return jnp.concatenate([rows, halo], axis=0)


def conv_kernel(
    at_ref, own, u1, u2, u3, u4, d1, d2, d3, d4, ab, r1, l1, r2, l2, other, bias_ref, perm_ref, out_ref,
    w_ref, x_ref, w_sem, x_sem,
):
    x, zh, y, core = at_ref[0], at_ref[1], at_ref[2], at_ref[3]
    copies = []

    def start(src, dst, sem):
        copy = pltpu.make_async_copy(src, dst, sem.at[len(copies)])
        copy.start()
        copies.append(copy)

    def rows_in(piece, chan, at):
        first = jnp.where(at == 0, 1, 5)
        beyond = jnp.where(at == 0, 0, 9)
        start(piece.at[pl.ds(0, 4)], x_ref.at[pl.ds(first, 4), :, chan], x_sem)
        start(piece.at[pl.ds(4, 1)], x_ref.at[pl.ds(beyond, 1), :, chan], x_sem)

    left, right, far = lax.rem(x + 3, 4), lax.rem(x + 1, 4), lax.rem(x + 2, 4)
    same, cross = zh, 1 - zh
    mine = [
        (ab.at[0], 2 * x + same), (ab.at[1], 2 * x + cross),
        (r1.at[0], 2 * left + same), (r1.at[1], 2 * left + cross),
        (l1.at[0], 2 * right + same), (l1.at[1], 2 * right + cross),
        (r2, 2 * far + same), (l2, 2 * far + cross),
    ]
    for n, (piece, chan) in enumerate(mine):
        rows_in(piece, chan, core)
        rows_in(other.at[n], chan, 1 - core)
    n_x = len(copies)
    for step, chunk in ((0, own), (7, u1), (6, u2), (5, u3), (1, d1), (2, d2), (3, d3)):
        start(chunk, w_ref.at[:, :, lax.rem(y + step, 8)], w_sem)
    opposite = lax.rem(y + 4, 8)
    start(u4, w_ref.at[:, :, opposite, :, pl.ds(0, 512)], w_sem)
    start(d4, w_ref.at[:, :, opposite, :, pl.ds(512, 512)], w_sem)
    for copy in copies:
        copy.wait()

    lane = lax.broadcasted_iota(jnp.int32, (128, 128), 1)

    def step(n, carry):
        pair, frame = n // 2, lax.rem(n, 2)
        total = jnp.zeros((384, 256), jnp.float32)
        for b in range(3):
            sides = []
            for q in range(2):
                row = 2 * pair + q + b
                parts = []
                for chan in range(8):
                    parts.append(x_ref[row, 0, chan])
                    parts.append(x_ref[row, frame, chan])
                sides.append(jnp.concatenate(parts, axis=0))
            taps = w_ref[b].reshape(384, 1024)
            total += jnp.dot(taps, jnp.concatenate(sides, axis=1), preferred_element_type=jnp.float32)
        for q in range(2):
            half = total[:, q * 128 : (q + 1) * 128]
            before = jnp.where(lane == 0, 0.0, pltpu.roll(half[:128], 1, 1))
            after = jnp.where(lane == 127, 0.0, pltpu.roll(half[256:], 127, 1))
            conv = before + half[128:256] + after + bias_ref[...]
            conv = conv.reshape(8, 2, 8, 128)
            both = jnp.concatenate([conv[:, 0].reshape(64, 128), conv[:, 1].reshape(64, 128)], axis=1)
            mixed = jnp.dot(both.astype(jnp.bfloat16), perm_ref[...], preferred_element_type=jnp.float32)
            out_ref[2 * pair + q, frame] = mixed.astype(jnp.bfloat16)
        return carry

    lax.fori_loop(0, 8, step, 0)


def convolve(at, chunks, pieces, bias, perm):
    n_any = len(chunks) + len(pieces)
    return pl.pallas_call(
        conv_kernel,
        out_shape=jax.ShapeDtypeStruct((8, 2, 64, 256), jnp.bfloat16),
        in_specs=[pl.BlockSpec(memory_space=pltpu.SMEM)]
        + [pl.BlockSpec(memory_space=pl.ANY)] * n_any
        + [pl.BlockSpec(memory_space=pltpu.VMEM)] * 2,
        out_specs=pl.BlockSpec(memory_space=pltpu.VMEM),
        scratch_shapes=[
            pltpu.VMEM((3, 3, 8, 16, 1024), jnp.bfloat16),
            pltpu.VMEM((10, 2, 8, 64, 128), jnp.bfloat16),
            pltpu.SemaphoreType.DMA((48,)),
            pltpu.SemaphoreType.DMA((48,)),
        ],
        compiler_params=pltpu.CompilerParams(vmem_limit_bytes=40 * 1024 * 1024),
        cost_estimate=pl.CostEstimate(flops=4_900_000_000, bytes_accessed=6_000_000, transcendentals=0),
        name="conv",
    )(at, *chunks, *pieces, bias, perm)


def local(latent, kernel, bias):
    x, zh, y, core = (lax.axis_index(a) for a in ("x", "zh", "y", "k"))
    own = own_chunk(kernel)
    up, down = ring(NY, 1), ring(NY, -1)
    u1 = lax.ppermute(own, "y", up)
    d1 = lax.ppermute(own, "y", down)
    u2 = lax.ppermute(u1, "y", up)
    d2 = lax.ppermute(d1, "y", down)
    u3 = lax.ppermute(u2, "y", up)
    d3 = lax.ppermute(d2, "y", down)
    u4 = lax.ppermute(u3[..., :512], "y", up)
    d4 = lax.ppermute(d3[..., 512:], "y", down)

    rows = own_rows(latent)
    ab = jnp.stack([rows, lax.ppermute(rows, "zh", ring(NH, 1))])
    r1 = lax.ppermute(ab, "x", ring(NX, 1))
    l1 = lax.ppermute(ab, "x", ring(NX, -1))
    r2 = lax.ppermute(r1[0], "x", ring(NX, 1))
    l2 = lax.ppermute(l1[1], "x", ring(NX, -1))
    other = lax.ppermute(jnp.concatenate([ab, r1, l1, r2[None], l2[None]]), "k", ring(NK, 1))

    split = bias.reshape(NY, NL, NK, NX, 2, NH, 2)
    picked = split[:, :, core, x, :, zh, :]
    column = jnp.transpose(picked, (0, 3, 1, 2)).reshape(128, 1)
    column = jnp.broadcast_to(column, (128, 128))
    place = jnp.arange(256)
    perm = (2 * (place % 128) + place // 128)[:, None] == place[None, :]
    at = jnp.stack([x, zh, y, core]).astype(jnp.int32)
    out = convolve(
        at, (own, u1, u2, u3, u4, d1, d2, d3, d4), (ab, r1, l1, r2, l2, other), column, perm.astype(jnp.bfloat16)
    )
    got = lax.all_to_all(out, ("k", "x"), 0, 0, tiled=True)
    got = got.reshape(NK, NX, 2, 32, 2, 256)
    return jnp.transpose(got, (2, 3, 0, 1, 4, 5)).reshape(2, 1, 512, 256)


def solution(mesh):
    fine = Mesh(mesh.devices.reshape(SIZES), AXES)
    tile = ("y", "zl", "k")
    chan = ("x", "zh")
    return jax.shard_map(
        local,
        mesh=fine,
        in_specs=(P(None, tile, chan, None), P(None, None, None, chan, tile), P()),
        out_specs=P(None, tile + chan, None, None),
        check_vma=False,
    )
```

```python
import functools

import jax
import jax.numpy as jnp
from jax import lax
from jax.experimental import pallas as pl
from jax.experimental.pallas import tpu as pltpu
from jax.sharding import Mesh, PartitionSpec as P

AXES = ("x", "zh", "y", "zl", "k")
SIZES = (4, 2, 8, 4, 2)
NX, NH, NY, NL, NK = SIZES


def ring(size, step):
    return [(i, (i + step) % size) for i in range(size)]


def spread_kernel(kernel):
    k01 = (kernel[0].astype(jnp.float32) + kernel[1].astype(jnp.float32)).astype(kernel.dtype)
    both = jnp.stack([k01, kernel[2]])
    split = both.reshape(2, 3, 3, 64, NX, 2, 2, 2)
    moved = jnp.transpose(split, (4, 6, 1, 2, 7, 5, 0, 3))
    flat = moved.reshape(NX, NH, 1, 3, 3, 2, 2, 128)
    return jnp.broadcast_to(flat, (NX, NH, NL, 3, 3, 2, 2, 128))


def own_chunk(kernel):
    pieces = spread_kernel(kernel).reshape(NX * NH * NL, 3, 3, 2, 2, 128)
    got = lax.all_to_all(pieces, ("x", "zh", "zl"), 0, 0, tiled=True)
    got = got.reshape(NX * NH, NL, 3, 3, 2, 2, 128)
    return jnp.transpose(got, (2, 3, 4, 1, 5, 0, 6)).reshape(3, 3, 16, 1024)


def own_rows(latent):
    core = lax.axis_index("k")
    rows = jnp.transpose(latent, (1, 0, 2, 3))
    edge = jnp.where(core == 0, rows[:1], rows[3:])
    pairs = [(2 * i + 1, 2 * i + 2) for i in range(31)]
    halo = lax.ppermute(edge, ("y", "zl", "k"), pairs + [(b, a) for a, b in pairs])
    return jnp.concatenate([rows, halo], axis=0)


def two_way(size):
    return [(2 * i + k, 2 * ((i + 1 - 2 * k) % size) + k) for i in range(size) for k in range(NK)]


def swap_cores(array):
    return lax.ppermute(array, "k", ring(NK, 1))


def conv_kernel(
    at_ref, both, c1, s1, c2, s2, c3, s3, c4, ab, e1, e1s, e2, e2s, bias_ref, perm_ref, out_ref,
    w_ref, x_ref, sems,
):
    x, zh, y, core = at_ref[0], at_ref[1], at_ref[2], at_ref[3]
    copies = []

    def start(src, dst):
        copy = pltpu.make_async_copy(src, dst, sems.at[len(copies)])
        copy.start()
        copies.append(copy)

    def rows_in(piece, x_from, owner):
        first = jnp.where(owner == 0, 1, 5)
        beyond = jnp.where(owner == 0, 0, 9)
        for j, chan in enumerate((2 * x_from + zh, 2 * x_from + 1 - zh)):
            start(piece.at[j, pl.ds(0, 4)], x_ref.at[pl.ds(first, 4), :, chan])
            start(piece.at[j, pl.ds(4, 1)], x_ref.at[pl.ds(beyond, 1), :, chan])

    there = 1 - core
    near, back = lax.rem(x + 3 + 2 * core, 4), lax.rem(x + 1 + 2 * core, 4)
    far = lax.rem(x + 2, 4)
    rows_in(ab.at[0], x, core)
    rows_in(ab.at[1], x, there)
    rows_in(e1.at[0], near, core)
    rows_in(e1.at[1], near, there)
    rows_in(e1s.at[0], back, there)
    rows_in(e1s.at[1], back, core)
    rows_in(e2, far, core)
    rows_in(e2s, far, there)
    sign = 1 - 2 * core
    start(both.at[0], w_ref.at[:, :, y])
    for n, (chunk, swapped) in enumerate(((c1, s1), (c2, s2), (c3, s3))):
        start(chunk.at[0], w_ref.at[:, :, lax.rem(y + 8 - (n + 1) * sign, 8)])
        start(swapped, w_ref.at[:, :, lax.rem(y + 8 + (n + 1) * sign, 8)])
    start(c4, w_ref.at[:, :, lax.rem(y + 4, 8)])
    for copy in copies:
        copy.wait()

    lane = lax.broadcasted_iota(jnp.int32, (128, 128), 1)

    def step(n, carry):
        pair, frame = n // 2, lax.rem(n, 2)
        total = jnp.zeros((384, 256), jnp.float32)
        for b in range(3):
            sides = []
            for q in range(2):
                row = 2 * pair + q + b
                parts = []
                for chan in range(8):
                    parts.append(x_ref[row, 0, chan])
                    parts.append(x_ref[row, frame, chan])
                sides.append(jnp.concatenate(parts, axis=0))
            taps = w_ref[b].reshape(384, 1024)
            total += jnp.dot(taps, jnp.concatenate(sides, axis=1), preferred_element_type=jnp.float32)
        for q in range(2):
            half = total[:, q * 128 : (q + 1) * 128]
            before = jnp.where(lane == 0, 0.0, pltpu.roll(half[:128], 1, 1))
            after = jnp.where(lane == 127, 0.0, pltpu.roll(half[256:], 127, 1))
            conv = before + half[128:256] + after + bias_ref[...]
            conv = conv.reshape(8, 2, 8, 128)
            both = jnp.concatenate([conv[:, 0].reshape(64, 128), conv[:, 1].reshape(64, 128)], axis=1)
            mixed = jnp.dot(both.astype(jnp.bfloat16), perm_ref[...], preferred_element_type=jnp.float32)
            out_ref[2 * pair + q, frame] = mixed.astype(jnp.bfloat16)
        return carry

    lax.fori_loop(0, 8, step, 0)


def convolve(at, chunks, pieces, bias, perm):
    n_any = len(chunks) + len(pieces)
    return pl.pallas_call(
        conv_kernel,
        out_shape=jax.ShapeDtypeStruct((8, 2, 64, 256), jnp.bfloat16),
        in_specs=[pl.BlockSpec(memory_space=pltpu.SMEM)]
        + [pl.BlockSpec(memory_space=pl.ANY)] * n_any
        + [pl.BlockSpec(memory_space=pltpu.VMEM)] * 2,
        out_specs=pl.BlockSpec(memory_space=pltpu.VMEM),
        scratch_shapes=[
            pltpu.VMEM((3, 3, 8, 16, 1024), jnp.bfloat16),
            pltpu.VMEM((10, 2, 8, 64, 128), jnp.bfloat16),
            pltpu.SemaphoreType.DMA((40,)),
        ],
        compiler_params=pltpu.CompilerParams(vmem_limit_bytes=40 * 1024 * 1024),
        cost_estimate=pl.CostEstimate(flops=4_900_000_000, bytes_accessed=6_000_000, transcendentals=0),
        name="conv",
    )(at, *chunks, *pieces, bias, perm)


def local(latent, kernel, bias):
    x, zh, y, core = (lax.axis_index(a) for a in ("x", "zh", "y", "k"))
    rows = own_rows(latent)
    own = own_chunk(kernel)
    own, rows = lax.optimization_barrier((own, rows))

    both = jnp.stack([own, swap_cores(own)])
    c1 = lax.ppermute(both, ("y", "k"), two_way(NY))
    c2 = lax.ppermute(c1, ("y", "k"), two_way(NY))
    c3 = lax.ppermute(c2, ("y", "k"), two_way(NY))
    c4 = lax.ppermute(c3[0], ("y", "k"), two_way(NY))
    s1, s2, s3 = swap_cores(c1[1]), swap_cores(c2[1]), swap_cores(c3[1])

    rows = jnp.stack([rows, lax.ppermute(rows, "zh", ring(NH, 1))])
    ab = jnp.stack([rows, swap_cores(rows)])
    e1 = lax.ppermute(ab, ("x", "k"), two_way(NX))
    e2 = lax.ppermute(e1[0], ("x", "k"), two_way(NX))
    e1s, e2s = swap_cores(e1), swap_cores(e2)

    split = bias.reshape(NY, NL, NK, NX, 2, NH, 2)
    picked = split[:, :, core, x, :, zh, :]
    column = jnp.transpose(picked, (0, 3, 1, 2)).reshape(128, 1)
    column = jnp.broadcast_to(column, (128, 128))
    place = jnp.arange(256)
    perm = (2 * (place % 128) + place // 128)[:, None] == place[None, :]
    at = jnp.stack([x, zh, y, core]).astype(jnp.int32)
    out = convolve(
        at, (both, c1, s1, c2, s2, c3, s3, c4), (ab, e1, e1s, e2, e2s), column, perm.astype(jnp.bfloat16)
    )
    got = lax.all_to_all(out, ("k", "x"), 0, 0, tiled=True)
    got = got.reshape(NK, NX, 2, 32, 2, 256)
    return jnp.transpose(got, (2, 3, 0, 1, 4, 5)).reshape(2, 1, 512, 256)


def solution(mesh):
    fine = Mesh(mesh.devices.reshape(SIZES), AXES)
    tile = ("y", "zl", "k")
    chan = ("x", "zh")
    return jax.shard_map(
        local,
        mesh=fine,
        in_specs=(P(None, tile, chan, None), P(None, None, None, chan, tile), P()),
        out_specs=P(None, tile + chan, None, None),
        check_vma=False,
    )
```

```python
import jax
import jax.numpy as jnp
from jax import lax
from jax.experimental import pallas as pl
from jax.experimental.pallas import tpu as pltpu
from jax.sharding import Mesh, PartitionSpec as P

AXES = ("x", "zh", "y", "zl", "k")
SIZES = (4, 2, 8, 4, 2)
NX, NH, NY, NL, NK = SIZES


def ring(size, step):
    return [(i, (i + step) % size) for i in range(size)]


def two_way(size):
    return [(2 * i + k, 2 * ((i + 1 - 2 * k) % size) + k) for i in range(size) for k in range(NK)]


def swap_cores(array):
    return lax.ppermute(array, "k", ring(NK, 1))


def spread_kernel(kernel):
    k01 = (kernel[0].astype(jnp.float32) + kernel[1].astype(jnp.float32)).astype(kernel.dtype)
    both = jnp.stack([k01, kernel[2]])
    split = both.reshape(2, 3, 3, 64, NX, 2, 2, 2)
    moved = jnp.transpose(split, (4, 6, 1, 2, 7, 5, 0, 3))
    flat = moved.reshape(NX, NH, 1, 3, 3, 2, 2, 128)
    return jnp.broadcast_to(flat, (NX, NH, NL, 3, 3, 2, 2, 128))


def own_chunk(kernel):
    pieces = spread_kernel(kernel).reshape(NX * NH * NL, 3, 3, 2, 2, 128)
    got = lax.all_to_all(pieces, ("x", "zh", "zl"), 0, 0, tiled=True)
    got = got.reshape(NX * NH, NL, 3, 3, 2, 2, 128)
    return jnp.transpose(got, (2, 3, 4, 1, 5, 0, 6)).reshape(3, 3, 16, 1024)


def own_rows(latent):
    rows = jnp.transpose(latent, (1, 0, 2, 3))
    edge = jnp.where(lax.axis_index("k") == 0, rows[:1], rows[3:])
    pairs = [(2 * i + 1, 2 * i + 2) for i in range(31)]
    halo = lax.ppermute(edge, ("y", "zl", "k"), pairs + [(b, a) for a, b in pairs])
    return jnp.concatenate([rows, halo], axis=0)


def conv_kernel(
    at_ref, mine, other, both, c1, s1, c2, s2, c3, s3, c4, bias_ref, perm_ref, out_ref, w_ref, x_ref, sems
):
    zh, core, y = at_ref[0], at_ref[1], at_ref[2]
    copies = []

    def start(src, dst):
        copy = pltpu.make_async_copy(src, dst, sems.at[len(copies)])
        copy.start()
        copies.append(copy)

    for piece, owner in ((mine, core), (other, 1 - core)):
        top = jnp.where(owner == 0, 1, 5)
        edge = jnp.where(owner == 0, 0, 9)
        for x in range(NX):
            for j in range(2):
                chan = 2 * x + (zh if j == 0 else 1 - zh)
                start(piece.at[x, j, pl.ds(0, 4)], x_ref.at[pl.ds(top, 4), :, chan])
                start(piece.at[x, j, pl.ds(4, 1)], x_ref.at[pl.ds(edge, 1), :, chan])
    sign = 1 - 2 * core
    start(both.at[0], w_ref.at[:, :, y])
    for n, (chunk, swapped) in enumerate(((c1, s1), (c2, s2), (c3, s3))):
        start(chunk.at[0], w_ref.at[:, :, lax.rem(y + 8 - (n + 1) * sign, 8)])
        start(swapped, w_ref.at[:, :, lax.rem(y + 8 + (n + 1) * sign, 8)])
    start(c4, w_ref.at[:, :, lax.rem(y + 4, 8)])
    for copy in copies:
        copy.wait()

    lane = lax.broadcasted_iota(jnp.int32, (128, 128), 1)

    def step(n, carry):
        pair, frame = n // 2, lax.rem(n, 2)
        total = jnp.zeros((384, 256), jnp.float32)
        for b in range(3):
            sides = []
            for q in range(2):
                row = 2 * pair + q + b
                parts = []
                for chan in range(8):
                    parts.append(x_ref[row, 0, chan])
                    parts.append(x_ref[row, frame, chan])
                sides.append(jnp.concatenate(parts, axis=0))
            taps = w_ref[b].reshape(384, 1024)
            total += jnp.dot(taps, jnp.concatenate(sides, axis=1), preferred_element_type=jnp.float32)
        for q in range(2):
            half = total[:, q * 128 : (q + 1) * 128]
            before = jnp.where(lane == 0, 0.0, pltpu.roll(half[:128], 1, 1))
            after = jnp.where(lane == 127, 0.0, pltpu.roll(half[256:], 127, 1))
            conv = before + half[128:256] + after + bias_ref[...]
            conv = conv.reshape(8, 2, 8, 128)
            both = jnp.concatenate([conv[:, 0].reshape(64, 128), conv[:, 1].reshape(64, 128)], axis=1)
            mixed = jnp.dot(both.astype(jnp.bfloat16), perm_ref[...], preferred_element_type=jnp.float32)
            out_ref[2 * pair + q, frame] = mixed.astype(jnp.bfloat16)
        return carry

    lax.fori_loop(0, 8, step, 0)


def convolve(at, rows, chunks, bias, perm):
    return pl.pallas_call(
        conv_kernel,
        out_shape=jax.ShapeDtypeStruct((8, 2, 64, 256), jnp.bfloat16),
        in_specs=[pl.BlockSpec(memory_space=pltpu.SMEM)]
        + [pl.BlockSpec(memory_space=pl.ANY)] * 10
        + [pl.BlockSpec(memory_space=pltpu.VMEM)] * 2,
        out_specs=pl.BlockSpec(memory_space=pltpu.VMEM),
        scratch_shapes=[
            pltpu.VMEM((3, 3, NY, 16, 1024), jnp.bfloat16),
            pltpu.VMEM((10, 2, 8, 64, 128), jnp.bfloat16),
            pltpu.SemaphoreType.DMA((40,)),
        ],
        compiler_params=pltpu.CompilerParams(vmem_limit_bytes=32 * 1024 * 1024),
        cost_estimate=pl.CostEstimate(flops=4_900_000_000, bytes_accessed=6_000_000, transcendentals=0),
        name="conv",
    )(at, *rows, *chunks, bias, perm)


def local(latent, kernel, bias):
    x, zh, y, core = (lax.axis_index(a) for a in ("x", "zh", "y", "k"))
    picked = bias.reshape(NY, NL, NK, NX, 2, NH, 2)[:, :, core, x, :, zh, :]
    column = jnp.transpose(picked, (0, 3, 1, 2)).reshape(128, 1)
    column = jnp.broadcast_to(column, (128, 128))
    rows = own_rows(latent)
    own = own_chunk(kernel)
    own, rows, column = lax.optimization_barrier((own, rows, column))

    both = jnp.stack([own, swap_cores(own)])
    c1 = lax.ppermute(both, ("y", "k"), two_way(NY))
    rows = jnp.stack([rows, lax.ppermute(rows, "zh", ring(NH, 1))])
    c1, rows = lax.optimization_barrier((c1, rows))
    c2 = lax.ppermute(c1, ("y", "k"), two_way(NY))
    mine = lax.all_to_all(jnp.broadcast_to(rows, (NX, *rows.shape)), "x", 0, 0, tiled=True)
    s1 = swap_cores(c1[1])
    c3 = lax.ppermute(c2, ("y", "k"), two_way(NY))
    s2 = swap_cores(c2[1])
    c3, mine, s1, s2 = lax.optimization_barrier((c3, mine, s1, s2))
    c4 = lax.ppermute(c3[0], ("y", "k"), two_way(NY))
    other = swap_cores(mine)
    s3 = swap_cores(c3[1])

    place = jnp.arange(256)
    perm = ((2 * (place % 128) + place // 128)[:, None] == place[None, :]).astype(jnp.bfloat16)
    at = jnp.stack([zh, core, y]).astype(jnp.int32)
    out = convolve(at, (mine, other), (both, c1, s1, c2, s2, c3, s3, c4), column, perm)
    got = lax.all_to_all(out, ("k", "x"), 0, 0, tiled=True).reshape(NK, NX, 2, NY * NL, 2, 256)
    return jnp.transpose(got, (2, 3, 0, 1, 4, 5)).reshape(2, 1, 512, 256)


def solution(mesh):
    fine = Mesh(mesh.devices.reshape(SIZES), AXES)
    tile = ("y", "zl", "k")
    chan = ("x", "zh")
    return jax.shard_map(
        local,
        mesh=fine,
        in_specs=(P(None, tile, chan, None), P(None, None, None, chan, tile), P()),
        out_specs=P(None, tile + chan, None, None),
        check_vma=False,
    )
```

```python
import jax
import jax.numpy as jnp
from jax import lax
from jax.experimental import pallas as pl
from jax.experimental.pallas import tpu as pltpu
from jax.sharding import Mesh, PartitionSpec as P

AXES = ("x1", "x0", "zh", "y", "zl1", "zl0", "k")
SIZES = (2, 2, 2, 8, 2, 2, 2)
NY = 8
ROWS = 4


def ring(size, step):
    return [(i, (i + step) % size) for i in range(size)]


def two_way(size):
    return [(2 * i + k, 2 * ((i + 1 - 2 * k) % size) + k) for i in range(size) for k in range(2)]


def swap(array, axis):
    return lax.ppermute(array, axis, ring(2, 1))


def spread_kernel(kernel):
    k01 = (kernel[0].astype(jnp.float32) + kernel[1].astype(jnp.float32)).astype(kernel.dtype)
    both = jnp.stack([k01, kernel[2]])
    split = both.reshape(2, 3, 3, 64, 2, 2, 2, 2, 2)
    moved = jnp.transpose(split, (4, 7, 5, 1, 2, 8, 6, 0, 3))
    flat = moved.reshape(2, 2, 1, 2, 3, 3, 2, 2, 128)
    return jnp.broadcast_to(flat, (2, 2, 2, 2, 3, 3, 2, 2, 128))


def own_chunk(kernel):
    pieces = spread_kernel(kernel).reshape(16, 3, 3, 2, 2, 128)
    got = lax.all_to_all(pieces, ("x0", "zh", "zl1", "zl0"), 0, 0, tiled=True)
    got = got.reshape(4, 4, 3, 3, 2, 2, 128)
    return jnp.transpose(got, (3, 4, 1, 5, 2, 0, 6)).reshape(3, 16, 1536)


def own_rows(latent):
    rows = jnp.transpose(latent, (1, 0, 2, 3))
    tile = ("y", "zl1", "zl0", "k")
    up = [(i, i + 1) for i in range(63)]
    above = lax.ppermute(rows[3:], tile, up)
    below = lax.ppermute(rows[:1], tile, [(b, a) for a, b in up])
    return jnp.concatenate([above, rows, below], axis=0)


def conv_kernel(
    at_ref, rows, both, c1, s1, c2, s2, c3, s3, c4, s4, bias_ref, perm_ref, out_ref,
    w_ref, x_ref, even_ref, odd_ref, sems,
):
    y, core = at_ref[0], at_ref[1]
    copies = []

    def start(src, dst):
        copy = pltpu.make_async_copy(src, dst, sems.at[len(copies)])
        copy.start()
        copies.append(copy)

    for x in range(2):
        for h in range(2):
            for z in range(2):
                start(rows.at[x, h, z], x_ref.at[z, :, :, 2 * x + h])
    sign = 1 - 2 * core
    for half, owner in enumerate((core, 1 - core)):
        start(both.at[half], w_ref.at[:, y, owner])
        for n, (chunk, swapped) in enumerate(((c1, s1), (c2, s2), (c3, s3))):
            start(chunk.at[half], w_ref.at[:, lax.rem(y + 8 - (n + 1) * sign, 8), owner])
            start(swapped.at[half], w_ref.at[:, lax.rem(y + 8 + (n + 1) * sign, 8), 1 - owner])
        start((c4, s4)[half], w_ref.at[:, lax.rem(y + 4, 8), owner])
    for copy in copies:
        copy.wait()

    lane = lax.broadcasted_iota(jnp.int32, (256, 128), 1)
    count = 8 // ROWS

    def place(n):
        part = lax.rem(n, count)
        return part * ROWS // 4, lax.rem(part * ROWS, 4), n // count

    def product(n):
        z, row, frame = place(n)
        sides = []
        for q in range(ROWS):
            parts = []
            for b in range(3):
                for chan in range(4):
                    parts.append(x_ref[z, row + q + b, 0, chan])
                    parts.append(x_ref[z, row + q + b, frame, chan])
            sides.append(jnp.concatenate(parts, axis=0))
        taps = w_ref[...].reshape(768, 1536)
        return jnp.dot(taps, jnp.concatenate(sides, axis=1), preferred_element_type=jnp.float32)

    def finish(total_ref, n):
        z, row, frame = place(n)
        mixed = []
        for q in range(ROWS):
            lanes = pl.ds(q * 128, 128)
            before = jnp.where(lane == 0, 0.0, pltpu.roll(total_ref[:256, lanes], 1, 1))
            after = jnp.where(lane == 127, 0.0, pltpu.roll(total_ref[512:, lanes], 127, 1))
            conv = before + total_ref[256:512, lanes] + after + bias_ref[...]
            conv = conv.reshape(16, 2, 8, 128)
            mixed.append(jnp.concatenate([conv[:, 0].reshape(128, 128), conv[:, 1].reshape(128, 128)], axis=1))
        mixed = jnp.concatenate(mixed, axis=0).astype(jnp.bfloat16)
        mixed = jnp.dot(mixed, perm_ref[...], preferred_element_type=jnp.float32).astype(jnp.bfloat16)
        for q in range(ROWS):
            out_ref[4 * z + row + q, frame] = mixed[128 * q : 128 * q + 128]

    def step(i, carry):
        n = 2 * i
        first = product(n)
        finish(odd_ref, jnp.maximum(n - 1, 0))
        even_ref[...] = first
        second = product(n + 1)
        finish(even_ref, n)
        odd_ref[...] = second
        return carry

    lax.fori_loop(0, count, step, 0)
    finish(odd_ref, 2 * count - 1)


def convolve(at, rows, chunks, bias, perm):
    return pl.pallas_call(
        conv_kernel,
        out_shape=jax.ShapeDtypeStruct((8, 2, 128, 256), jnp.bfloat16),
        in_specs=[pl.BlockSpec(memory_space=pltpu.SMEM)]
        + [pl.BlockSpec(memory_space=pl.ANY)] * 10
        + [pl.BlockSpec(memory_space=pltpu.VMEM)] * 2,
        out_specs=pl.BlockSpec(memory_space=pltpu.VMEM),
        scratch_shapes=[
            pltpu.VMEM((3, NY, 2, 16, 1536), jnp.bfloat16),
            pltpu.VMEM((2, 6, 2, 4, 64, 128), jnp.bfloat16),
            pltpu.VMEM((768, 128 * ROWS), jnp.float32),
            pltpu.VMEM((768, 128 * ROWS), jnp.float32),
            pltpu.SemaphoreType.DMA((24,)),
        ],
        compiler_params=pltpu.CompilerParams(vmem_limit_bytes=36 * 1024 * 1024),
        cost_estimate=pl.CostEstimate(flops=4_900_000_000, bytes_accessed=6_000_000, transcendentals=0),
        name="conv",
    )(at, rows, *chunks, bias, perm)


def local(latent, kernel, bias):
    x1, x0, zh, y, core = (lax.axis_index(a) for a in ("x1", "x0", "zh", "y", "k"))
    zl0 = lax.axis_index("zl0")
    picked = bias.reshape(NY, 4, 2, 2, 2, 2, 2, 2)[:, :, :, x0, zl0, :, zh, :]
    column = jnp.transpose(picked, (0, 2, 4, 1, 3)).reshape(256, 1)
    column = jnp.broadcast_to(jnp.where(x1 == 0, column, 0.0), (256, 128))
    rows = own_rows(latent)
    own = own_chunk(kernel)
    own, rows, column = lax.optimization_barrier((own, rows, column))

    both = jnp.stack([own, swap(own, "k")])
    both, rows = lax.optimization_barrier((both, rows))
    c1 = lax.ppermute(both, ("y", "k"), two_way(NY))
    rows = lax.all_to_all(jnp.broadcast_to(rows, (8, *rows.shape)), ("x0", "zh", "zl0"), 0, 0, tiled=True)
    rows = rows.reshape(2, 2, 2, *rows.shape[1:])
    c2 = lax.ppermute(c1, ("y", "k"), two_way(NY))
    s1 = swap(c1, "k")
    c3 = lax.ppermute(c2, ("y", "k"), two_way(NY))
    s2 = swap(c2, "k")
    c3, s1, s2 = lax.optimization_barrier((c3, s1, s2))
    c4 = lax.ppermute(c3[0], ("y", "k"), two_way(NY))
    s3 = swap(c3, "k")
    s4 = swap(c4, "k")

    place = jnp.arange(256)
    perm = ((2 * (place % 128) + place // 128)[:, None] == place[None, :]).astype(jnp.bfloat16)
    at = jnp.stack([y, core]).astype(jnp.int32)
    out = convolve(at, rows, (both, c1, s1, c2, s2, c3, s3, c4, s4), column, perm)
    got = lax.all_to_all(out, ("zl0", "x1", "x0"), 0, 0, tiled=True).reshape(2, 2, 2, 2, NY, 2, 4, 2, 256)
    total = (got[:, 0].astype(jnp.float32) + got[:, 1].astype(jnp.float32)).astype(jnp.bfloat16)
    return jnp.transpose(total, (2, 3, 5, 4, 1, 0, 6, 7)).reshape(2, 1, 512, 256)


def solution(mesh):
    fine = Mesh(mesh.devices.reshape(SIZES), AXES)
    tile = ("y", "zl1", "zl0", "k")
    chan = ("x1", "x0", "zh")
    return jax.shard_map(
        local,
        mesh=fine,
        in_specs=(P(None, tile, chan, None), P(None, None, None, chan, tile), P()),
        out_specs=P(None, tile + chan, None, None),
        check_vma=False,
    )
```

```python
import jax
import jax.numpy as jnp
from jax import lax
from jax.experimental import pallas as pl
from jax.experimental.pallas import tpu as pltpu
from jax.sharding import Mesh, PartitionSpec as P

AXES = ("x1", "x0", "zh", "y", "zl1", "zl0", "k")
SIZES = (2, 2, 2, 8, 2, 2, 2)
NY = 8
ROWS = 4


def ring(size, step):
    return [(i, (i + step) % size) for i in range(size)]


def swap(array, axis):
    return lax.ppermute(array, axis, ring(2, 1))


def spread_kernel(kernel):
    k01 = (kernel[0].astype(jnp.float32) + kernel[1].astype(jnp.float32)).astype(kernel.dtype)
    both = jnp.stack([k01, kernel[2]])
    split = both.reshape(2, 3, 3, 64, 2, 2, 2, 2, 2)
    moved = jnp.transpose(split, (4, 7, 5, 1, 2, 8, 6, 0, 3))
    flat = moved.reshape(2, 2, 1, 2, 3, 3, 2, 2, 128)
    return jnp.broadcast_to(flat, (2, 2, 2, 2, 3, 3, 2, 2, 128))


def own_chunk(kernel):
    pieces = spread_kernel(kernel).reshape(16, 3, 3, 2, 2, 128)
    got = lax.all_to_all(pieces, ("x0", "zh", "zl1", "zl0"), 0, 0, tiled=True)
    got = got.reshape(4, 4, 3, 3, 2, 2, 128)
    return jnp.transpose(got, (3, 4, 1, 5, 2, 0, 6)).reshape(3, 16, 1536)


def own_rows(latent):
    rows = jnp.transpose(latent, (1, 0, 2, 3))
    tile = ("y", "zl1", "zl0", "k")
    up = [(i, i + 1) for i in range(63)]
    above = lax.ppermute(rows[3:], tile, up)
    below = lax.ppermute(rows[:1], tile, [(b, a) for a, b in up])
    return jnp.concatenate([above, rows, below], axis=0)


def conv_kernel(
    at_ref, here, over_x, over_z, over_both, mine, other, bias_ref, perm_ref, out_ref,
    w_ref, x_ref, even_ref, odd_ref, sems,
):
    x0, zh, zl0, core = (at_ref[n] for n in range(4))
    copies = []

    def start(src, dst):
        copy = pltpu.make_async_copy(src, dst, sems.at[len(copies)])
        copy.start()
        copies.append(copy)

    for rows, x, z in ((here, x0, zl0), (over_x, 1 - x0, zl0), (over_z, x0, 1 - zl0), (over_both, 1 - x0, 1 - zl0)):
        for n, h in enumerate((zh, 1 - zh)):
            start(rows.at[n], x_ref.at[z, :, :, 2 * x + h])
    for chunks, owner in ((mine, core), (other, 1 - core)):
        for y in range(NY):
            start(chunks.at[y], w_ref.at[:, y, owner])
    for copy in copies:
        copy.wait()

    lane = lax.broadcasted_iota(jnp.int32, (256, 128), 1)
    count = 8 // ROWS

    def place(n):
        part = lax.rem(n, count)
        return part * ROWS // 4, lax.rem(part * ROWS, 4), n // count

    def product(n):
        z, row, frame = place(n)
        sides = []
        for q in range(ROWS):
            parts = []
            for b in range(3):
                for chan in range(4):
                    parts.append(x_ref[z, row + q + b, 0, chan])
                    parts.append(x_ref[z, row + q + b, frame, chan])
            sides.append(jnp.concatenate(parts, axis=0))
        taps = w_ref[...].reshape(768, 1536)
        return jnp.dot(taps, jnp.concatenate(sides, axis=1), preferred_element_type=jnp.float32)

    def finish(total_ref, n):
        z, row, frame = place(n)
        mixed = []
        for q in range(ROWS):
            lanes = pl.ds(q * 128, 128)
            before = jnp.where(lane == 0, 0.0, pltpu.roll(total_ref[:256, lanes], 1, 1))
            after = jnp.where(lane == 127, 0.0, pltpu.roll(total_ref[512:, lanes], 127, 1))
            conv = before + total_ref[256:512, lanes] + after + bias_ref[...]
            conv = conv.reshape(16, 2, 8, 128)
            mixed.append(jnp.concatenate([conv[:, 0].reshape(128, 128), conv[:, 1].reshape(128, 128)], axis=1))
        mixed = jnp.concatenate(mixed, axis=0).astype(jnp.bfloat16)
        mixed = jnp.dot(mixed, perm_ref[...], preferred_element_type=jnp.float32).astype(jnp.bfloat16)
        for q in range(ROWS):
            out_ref[4 * z + row + q, frame] = mixed[128 * q : 128 * q + 128]

    def step(i, carry):
        n = 2 * i
        first = product(n)
        finish(odd_ref, jnp.maximum(n - 1, 0))
        even_ref[...] = first
        second = product(n + 1)
        finish(even_ref, n)
        odd_ref[...] = second
        return carry

    lax.fori_loop(0, count, step, 0)
    finish(odd_ref, 2 * count - 1)


def convolve(at, rows, chunks, bias, perm):
    return pl.pallas_call(
        conv_kernel,
        out_shape=jax.ShapeDtypeStruct((8, 2, 128, 256), jnp.bfloat16),
        in_specs=[pl.BlockSpec(memory_space=pltpu.SMEM)]
        + [pl.BlockSpec(memory_space=pl.ANY)] * 6
        + [pl.BlockSpec(memory_space=pltpu.VMEM)] * 2,
        out_specs=pl.BlockSpec(memory_space=pltpu.VMEM),
        scratch_shapes=[
            pltpu.VMEM((3, NY, 2, 16, 1536), jnp.bfloat16),
            pltpu.VMEM((2, 6, 2, 4, 64, 128), jnp.bfloat16),
            pltpu.VMEM((768, 128 * ROWS), jnp.float32),
            pltpu.VMEM((768, 128 * ROWS), jnp.float32),
            pltpu.SemaphoreType.DMA((24,)),
        ],
        compiler_params=pltpu.CompilerParams(vmem_limit_bytes=36 * 1024 * 1024),
        cost_estimate=pl.CostEstimate(flops=4_900_000_000, bytes_accessed=6_000_000, transcendentals=0),
        name="conv",
    )(at, *rows, *chunks, bias, perm)


def local(latent, kernel, bias):
    x1, x0, zh, zl0, core = (lax.axis_index(a) for a in ("x1", "x0", "zh", "zl0", "k"))
    picked = bias.reshape(NY, 4, 2, 2, 2, 2, 2, 2)[:, :, :, x0, zl0, :, zh, :]
    column = jnp.transpose(picked, (0, 2, 4, 1, 3)).reshape(256, 1)
    column = jnp.broadcast_to(jnp.where(x1 == 0, column, 0.0), (256, 128))
    rows = own_rows(latent)
    own = own_chunk(kernel)
    own, rows, column = lax.optimization_barrier((own, rows, column))

    mine = lax.all_to_all(jnp.broadcast_to(own, (NY, *own.shape)), "y", 0, 0, tiled=True)
    rows = jnp.stack([rows, swap(rows, "zh")])
    over_x, over_z = swap(rows, "x0"), swap(rows, "zl0")
    over_both = lax.ppermute(rows, ("x0", "zl0"), [(i, 3 - i) for i in range(4)])
    mine, rows, over_x, over_z, over_both = lax.optimization_barrier((mine, rows, over_x, over_z, over_both))
    other = swap(mine, "k")

    place = jnp.arange(256)
    perm = ((2 * (place % 128) + place // 128)[:, None] == place[None, :]).astype(jnp.bfloat16)
    at = jnp.stack([x0, zh, zl0, core]).astype(jnp.int32)
    out = convolve(at, (rows, over_x, over_z, over_both), (mine, other), column, perm)
    got = lax.all_to_all(out, ("zl0", "x1", "x0"), 0, 0, tiled=True).reshape(2, 2, 2, 2, NY, 2, 4, 2, 256)
    total = (got[:, 0].astype(jnp.float32) + got[:, 1].astype(jnp.float32)).astype(jnp.bfloat16)
    return jnp.transpose(total, (2, 3, 5, 4, 1, 0, 6, 7)).reshape(2, 1, 512, 256)


def solution(mesh):
    fine = Mesh(mesh.devices.reshape(SIZES), AXES)
    tile = ("y", "zl1", "zl0", "k")
    chan = ("x1", "x0", "zh")
    return jax.shard_map(
        local,
        mesh=fine,
        in_specs=(P(None, tile, chan, None), P(None, None, None, chan, tile), P()),
        out_specs=P(None, tile + chan, None, None),
        check_vma=False,
    )
```

```python
import jax
import jax.numpy as jnp
from jax import lax
from jax.experimental import pallas as pl
from jax.experimental.pallas import tpu as pltpu
from jax.sharding import Mesh, PartitionSpec as P

AXES = ("x1", "x0", "zh", "y", "zl1", "zl0", "k")
SIZES = (2, 2, 2, 8, 2, 2, 2)
NY = 8
ROWS = 4


def ring(size, step):
    return [(i, (i + step) % size) for i in range(size)]


def swap(array, axis):
    return lax.ppermute(array, axis, ring(2, 1))


def spread_kernel(kernel):
    k01 = (kernel[0].astype(jnp.float32) + kernel[1].astype(jnp.float32)).astype(kernel.dtype)
    both = jnp.stack([k01, kernel[2]])
    split = both.reshape(2, 3, 3, 64, 2, 2, 2, 2, 2)
    moved = jnp.transpose(split, (4, 7, 5, 1, 2, 8, 6, 0, 3))
    flat = moved.reshape(2, 2, 1, 2, 3, 3, 2, 2, 128)
    return jnp.broadcast_to(flat, (2, 2, 2, 2, 3, 3, 2, 2, 128))


def own_chunk(kernel):
    pieces = spread_kernel(kernel).reshape(16, 3, 3, 2, 2, 128)
    got = lax.all_to_all(pieces, ("x0", "zh", "zl1", "zl0"), 0, 0, tiled=True)
    got = got.reshape(4, 4, 3, 3, 2, 2, 128)
    return jnp.transpose(got, (3, 4, 1, 5, 2, 0, 6)).reshape(3, 16, 1536)


def own_rows(latent):
    rows = jnp.transpose(latent, (1, 0, 2, 3))
    tile = ("y", "zl1", "zl0", "k")
    up = [(i, i + 1) for i in range(63)]
    above = lax.ppermute(rows[3:], tile, up)
    below = lax.ppermute(rows[:1], tile, [(b, a) for a, b in up])
    return jnp.concatenate([above, rows, below], axis=0)


def start_copy(copies, sems, src, dst):
    copy = pltpu.make_async_copy(src, dst, sems.at[len(copies)])
    copy.start()
    copies.append(copy)


def pack_kernel(at_ref, here, over_x, over_z, over_both, x_ref, sems):
    x0, zh, zl0 = (at_ref[n] for n in range(3))
    copies = []
    for rows, x, z in ((here, x0, zl0), (over_x, 1 - x0, zl0), (over_z, x0, 1 - zl0), (over_both, 1 - x0, 1 - zl0)):
        for n, h in enumerate((zh, 1 - zh)):
            start_copy(copies, sems, rows.at[n], x_ref.at[z, :, :, 2 * x + h])
    for copy in copies:
        copy.wait()


def pack(at, rows):
    return pl.pallas_call(
        pack_kernel,
        out_shape=jax.ShapeDtypeStruct((2, 6, 2, 4, 64, 128), jnp.bfloat16),
        in_specs=[pl.BlockSpec(memory_space=pltpu.SMEM)] + [pl.BlockSpec(memory_space=pl.ANY)] * 4,
        out_specs=pl.BlockSpec(memory_space=pltpu.VMEM),
        scratch_shapes=[pltpu.SemaphoreType.DMA((8,))],
        compiler_params=pltpu.CompilerParams(vmem_limit_bytes=4 * 1024 * 1024),
        cost_estimate=pl.CostEstimate(flops=0, bytes_accessed=3_200_000, transcendentals=0),
        name="pack",
    )(at, *rows)


def conv_kernel(at_ref, x_ref, mine, other, bias_ref, perm_ref, out_ref, w_ref, even_ref, odd_ref, sems):
    core = at_ref[3]
    copies = []
    for chunks, owner in ((mine, core), (other, 1 - core)):
        for y in range(NY):
            start_copy(copies, sems, chunks.at[y], w_ref.at[:, y, owner])
    for copy in copies:
        copy.wait()

    lane = lax.broadcasted_iota(jnp.int32, (256, 128), 1)
    count = 8 // ROWS

    def place(n):
        part = lax.rem(n, count)
        return part * ROWS // 4, lax.rem(part * ROWS, 4), n // count

    def product(n):
        z, row, frame = place(n)
        sides = []
        for q in range(ROWS):
            parts = []
            for b in range(3):
                for chan in range(4):
                    parts.append(x_ref[z, row + q + b, 0, chan])
                    parts.append(x_ref[z, row + q + b, frame, chan])
            sides.append(jnp.concatenate(parts, axis=0))
        taps = w_ref[...].reshape(768, 1536)
        return jnp.dot(taps, jnp.concatenate(sides, axis=1), preferred_element_type=jnp.float32)

    def finish(total_ref, n):
        z, row, frame = place(n)
        mixed = []
        for q in range(ROWS):
            lanes = pl.ds(q * 128, 128)
            before = jnp.where(lane == 0, 0.0, pltpu.roll(total_ref[:256, lanes], 1, 1))
            after = jnp.where(lane == 127, 0.0, pltpu.roll(total_ref[512:, lanes], 127, 1))
            conv = before + total_ref[256:512, lanes] + after + bias_ref[...]
            conv = conv.reshape(16, 2, 8, 128)
            mixed.append(jnp.concatenate([conv[:, 0].reshape(128, 128), conv[:, 1].reshape(128, 128)], axis=1))
        mixed = jnp.concatenate(mixed, axis=0).astype(jnp.bfloat16)
        mixed = jnp.dot(mixed, perm_ref[...], preferred_element_type=jnp.float32).astype(jnp.bfloat16)
        for q in range(ROWS):
            out_ref[4 * z + row + q, frame] = mixed[128 * q : 128 * q + 128]

    def step(i, carry):
        n = 2 * i
        first = product(n)
        finish(odd_ref, jnp.maximum(n - 1, 0))
        even_ref[...] = first
        second = product(n + 1)
        finish(even_ref, n)
        odd_ref[...] = second
        return carry

    lax.fori_loop(0, count, step, 0)
    finish(odd_ref, 2 * count - 1)


def convolve(at, rows, chunks, bias, perm):
    return pl.pallas_call(
        conv_kernel,
        out_shape=jax.ShapeDtypeStruct((8, 2, 128, 256), jnp.bfloat16),
        in_specs=[pl.BlockSpec(memory_space=pltpu.SMEM)]
        + [pl.BlockSpec(memory_space=pltpu.VMEM)]
        + [pl.BlockSpec(memory_space=pl.ANY)] * 2
        + [pl.BlockSpec(memory_space=pltpu.VMEM)] * 2,
        out_specs=pl.BlockSpec(memory_space=pltpu.VMEM),
        scratch_shapes=[
            pltpu.VMEM((3, NY, 2, 16, 1536), jnp.bfloat16),
            pltpu.VMEM((768, 128 * ROWS), jnp.float32),
            pltpu.VMEM((768, 128 * ROWS), jnp.float32),
            pltpu.SemaphoreType.DMA((24,)),
        ],
        compiler_params=pltpu.CompilerParams(vmem_limit_bytes=18 * 1024 * 1024),
        cost_estimate=pl.CostEstimate(flops=4_900_000_000, bytes_accessed=6_000_000, transcendentals=0),
        name="conv",
    )(at, rows, *chunks, bias, perm)


def local(latent, kernel, bias):
    x1, x0, zh, zl0, core = (lax.axis_index(a) for a in ("x1", "x0", "zh", "zl0", "k"))
    picked = bias.reshape(NY, 4, 2, 2, 2, 2, 2, 2)[:, :, :, x0, zl0, :, zh, :]
    column = jnp.transpose(picked, (0, 2, 4, 1, 3)).reshape(256, 1)
    column = jnp.broadcast_to(jnp.where(x1 == 0, column, 0.0), (256, 128))
    rows = own_rows(latent)
    own = own_chunk(kernel)
    own, rows, column = lax.optimization_barrier((own, rows, column))

    mine = lax.all_to_all(jnp.broadcast_to(own, (NY, *own.shape)), "y", 0, 0, tiled=True)
    rows = jnp.stack([rows, swap(rows, "zh")])
    over_x, over_z = swap(rows, "x0"), swap(rows, "zl0")
    over_both = lax.ppermute(rows, ("x0", "zl0"), [(i, 3 - i) for i in range(4)])
    mine, rows, over_x, over_z, over_both = lax.optimization_barrier((mine, rows, over_x, over_z, over_both))
    at = jnp.stack([x0, zh, zl0, core]).astype(jnp.int32)
    packed = pack(at, (rows, over_x, over_z, over_both))
    other = swap(mine, "k")

    place = jnp.arange(256)
    perm = ((2 * (place % 128) + place // 128)[:, None] == place[None, :]).astype(jnp.bfloat16)
    out = convolve(at, packed, (mine, other), column, perm)
    got = lax.all_to_all(out, ("zl0", "x1", "x0"), 0, 0, tiled=True).reshape(2, 2, 2, 2, NY, 2, 4, 2, 256)
    total = (got[:, 0].astype(jnp.float32) + got[:, 1].astype(jnp.float32)).astype(jnp.bfloat16)
    return jnp.transpose(total, (2, 3, 5, 4, 1, 0, 6, 7)).reshape(2, 1, 512, 256)


def solution(mesh):
    fine = Mesh(mesh.devices.reshape(SIZES), AXES)
    tile = ("y", "zl1", "zl0", "k")
    chan = ("x1", "x0", "zh")
    return jax.shard_map(
        local,
        mesh=fine,
        in_specs=(P(None, tile, chan, None), P(None, None, None, chan, tile), P()),
        out_specs=P(None, tile + chan, None, None),
        check_vma=False,
    )
```

```python
import jax
import jax.numpy as jnp
from jax import lax
from jax.experimental import pallas as pl
from jax.experimental.pallas import tpu as pltpu
from jax.sharding import Mesh, PartitionSpec as P

AXES = ("x1", "x0", "zh", "y", "zl1", "zl0", "k")
SIZES = (2, 2, 2, 8, 2, 2, 2)
NY = 8
ROWS = 4


def ring(size, step):
    return [(i, (i + step) % size) for i in range(size)]


def swap(array, axis):
    return lax.ppermute(array, axis, ring(2, 1))


def spread_kernel(kernel):
    k01 = (kernel[0].astype(jnp.float32) + kernel[1].astype(jnp.float32)).astype(kernel.dtype)
    both = jnp.stack([k01, kernel[2]])
    split = both.reshape(2, 3, 3, 64, 2, 2, 2, 2, 2)
    moved = jnp.transpose(split, (4, 7, 5, 1, 2, 8, 6, 0, 3))
    flat = moved.reshape(2, 2, 1, 2, 3, 3, 2, 2, 128)
    return jnp.broadcast_to(flat, (2, 2, 2, 2, 3, 3, 2, 2, 128))


def own_chunk(kernel):
    pieces = spread_kernel(kernel).reshape(16, 3, 3, 2, 2, 128)
    got = lax.all_to_all(pieces, ("x0", "zh", "zl1", "zl0"), 0, 0, tiled=True)
    got = got.reshape(4, 4, 3, 3, 2, 2, 128)
    return jnp.transpose(got, (3, 4, 1, 5, 2, 0, 6)).reshape(3, 16, 1536)


def own_rows(latent):
    rows = jnp.transpose(latent, (1, 0, 2, 3))
    tile = ("y", "zl1", "zl0", "k")
    up = [(i, i + 1) for i in range(63)]
    above = lax.ppermute(rows[3:], tile, up)
    below = lax.ppermute(rows[:1], tile, [(b, a) for a, b in up])
    return jnp.concatenate([above, rows, below], axis=0)


def start_copy(copies, sems, src, dst):
    copy = pltpu.make_async_copy(src, dst, sems.at[len(copies)])
    copy.start()
    copies.append(copy)


def pack_kernel(at_ref, here, over_x, over_z, over_both, x_ref, sems):
    x0, zh, zl0 = (at_ref[n] for n in range(3))
    copies = []
    for rows, x, z in ((here, x0, zl0), (over_x, 1 - x0, zl0), (over_z, x0, 1 - zl0), (over_both, 1 - x0, 1 - zl0)):
        for n, h in enumerate((zh, 1 - zh)):
            start_copy(copies, sems, rows.at[n], x_ref.at[z, :, :, 2 * x + h])
    for copy in copies:
        copy.wait()


def pack(at, rows):
    return pl.pallas_call(
        pack_kernel,
        out_shape=jax.ShapeDtypeStruct((2, 6, 2, 4, 64, 128), jnp.bfloat16),
        in_specs=[pl.BlockSpec(memory_space=pltpu.SMEM)] + [pl.BlockSpec(memory_space=pl.ANY)] * 4,
        out_specs=pl.BlockSpec(memory_space=pltpu.VMEM),
        scratch_shapes=[pltpu.SemaphoreType.DMA((8,))],
        compiler_params=pltpu.CompilerParams(vmem_limit_bytes=4 * 1024 * 1024),
        cost_estimate=pl.CostEstimate(flops=0, bytes_accessed=3_200_000, transcendentals=0),
        name="pack",
    )(at, *rows)


def conv_kernel(at_ref, x_ref, mine, other, bias_ref, perm_ref, out_ref, even_ref, odd_ref):
    first = at_ref[3] == 0
    lane = lax.broadcasted_iota(jnp.int32, (256, 128), 1)
    count = 8 // ROWS

    def place(n):
        part = lax.rem(n, count)
        return part * ROWS // 4, lax.rem(part * ROWS, 4), n // count

    def product(n):
        z, row, frame = place(n)
        sides = []
        for q in range(ROWS):
            parts = []
            for b in range(3):
                for chan in range(4):
                    parts.append(x_ref[z, row + q + b, 0, chan])
                    parts.append(x_ref[z, row + q + b, frame, chan])
            sides.append(jnp.concatenate(parts, axis=0))
        taps = [half[y, c] for c in range(3) for y in range(NY) for half in (mine, other)]
        taps = jnp.concatenate(taps, axis=0)
        return jnp.dot(taps, jnp.concatenate(sides, axis=1), preferred_element_type=jnp.float32)

    def finish(total_ref, n):
        z, row, frame = place(n)
        mixed = []
        for q in range(ROWS):
            lanes = pl.ds(q * 128, 128)
            before = jnp.where(lane == 0, 0.0, pltpu.roll(total_ref[:256, lanes], 1, 1))
            after = jnp.where(lane == 127, 0.0, pltpu.roll(total_ref[512:, lanes], 127, 1))
            conv = before + total_ref[256:512, lanes] + after + bias_ref[...]
            conv = conv.reshape(NY, 2, 2, 8, 128)
            conv = jnp.where(first, conv, jnp.concatenate([conv[:, 1:], conv[:, :1]], axis=1))
            mixed.append(jnp.concatenate([conv[:, :, s].reshape(128, 128) for s in range(2)], axis=1))
        mixed = jnp.concatenate(mixed, axis=0).astype(jnp.bfloat16)
        mixed = jnp.dot(mixed, perm_ref[...], preferred_element_type=jnp.float32).astype(jnp.bfloat16)
        for q in range(ROWS):
            out_ref[4 * z + row + q, frame] = mixed[128 * q : 128 * q + 128]

    def step(i, carry):
        n = 2 * i
        first = product(n)
        finish(odd_ref, jnp.maximum(n - 1, 0))
        even_ref[...] = first
        second = product(n + 1)
        finish(even_ref, n)
        odd_ref[...] = second
        return carry

    lax.fori_loop(0, count, step, 0)
    finish(odd_ref, 2 * count - 1)


def convolve(at, rows, chunks, bias, perm):
    return pl.pallas_call(
        conv_kernel,
        out_shape=jax.ShapeDtypeStruct((8, 2, 128, 256), jnp.bfloat16),
        in_specs=[pl.BlockSpec(memory_space=pltpu.SMEM)]
        + [pl.BlockSpec(memory_space=pltpu.VMEM)] * 5,
        out_specs=pl.BlockSpec(memory_space=pltpu.VMEM),
        scratch_shapes=[
            pltpu.VMEM((768, 128 * ROWS), jnp.float32),
            pltpu.VMEM((768, 128 * ROWS), jnp.float32),
        ],
        compiler_params=pltpu.CompilerParams(vmem_limit_bytes=18 * 1024 * 1024),
        cost_estimate=pl.CostEstimate(flops=4_900_000_000, bytes_accessed=6_000_000, transcendentals=0),
        name="conv",
    )(at, rows, *chunks, bias, perm)


def local(latent, kernel, bias):
    x1, x0, zh, zl0, core = (lax.axis_index(a) for a in ("x1", "x0", "zh", "zl0", "k"))
    picked = bias.reshape(NY, 4, 2, 2, 2, 2, 2, 2)[:, :, :, x0, zl0, :, zh, :]
    picked = jnp.where(core == 0, picked, picked[:, :, ::-1])
    column = jnp.transpose(picked, (0, 2, 4, 1, 3)).reshape(256, 1)
    column = jnp.broadcast_to(jnp.where(x1 == 0, column, 0.0), (256, 128))
    rows = own_rows(latent)
    own = own_chunk(kernel)
    own, rows, column = lax.optimization_barrier((own, rows, column))

    mine = lax.all_to_all(jnp.broadcast_to(own, (NY, *own.shape)), "y", 0, 0, tiled=True)
    rows = jnp.stack([rows, swap(rows, "zh")])
    over_x, over_z = swap(rows, "x0"), swap(rows, "zl0")
    over_both = lax.ppermute(rows, ("x0", "zl0"), [(i, 3 - i) for i in range(4)])
    mine, rows, over_x, over_z, over_both = lax.optimization_barrier((mine, rows, over_x, over_z, over_both))
    at = jnp.stack([x0, zh, zl0, core]).astype(jnp.int32)
    packed = pack(at, (rows, over_x, over_z, over_both))
    other = swap(mine, "k")

    place = jnp.arange(256)
    perm = ((2 * (place % 128) + place // 128)[:, None] == place[None, :]).astype(jnp.bfloat16)
    out = convolve(at, packed, (mine, other), column, perm)
    got = lax.all_to_all(out, ("zl0", "x1", "x0"), 0, 0, tiled=True).reshape(2, 2, 2, 2, 128, 256)
    total = (got[:, 0].astype(jnp.float32) + got[:, 1].astype(jnp.float32)).astype(jnp.bfloat16)
    total = total.reshape(2, 2, 2, NY, 2, 4, 2, 256)
    return jnp.transpose(total, (2, 3, 5, 4, 1, 0, 6, 7)).reshape(2, 1, 512, 256)


def solution(mesh):
    fine = Mesh(mesh.devices.reshape(SIZES), AXES)
    tile = ("y", "zl1", "zl0", "k")
    chan = ("x1", "x0", "zh")
    return jax.shard_map(
        local,
        mesh=fine,
        in_specs=(P(None, tile, chan, None), P(None, None, None, chan, tile), P()),
        out_specs=P(None, tile + chan, None, None),
        check_vma=False,
    )
```

```python
import jax
import jax.numpy as jnp
from jax import lax
from jax.experimental import pallas as pl
from jax.experimental.pallas import tpu as pltpu
from jax.sharding import Mesh, PartitionSpec as P

AXES = ("x1", "x0", "zh", "y", "zl1", "zl0", "k")
SIZES = (2, 2, 2, 8, 2, 2, 2)
NY = 8
ROWS = 4


def ring(size, step):
    return [(i, (i + step) % size) for i in range(size)]


def swap(array, axis):
    return lax.ppermute(array, axis, ring(2, 1))


def sum_kernel(taps_ref, out_ref):
    for b in range(3):
        for c in range(3):
            k01 = taps_ref[0, b, c].astype(jnp.float32) + taps_ref[1, b, c].astype(jnp.float32)
            k2 = taps_ref[2, b, c].astype(jnp.float32)
            out_ref[b, c] = jnp.concatenate([k01, k2], axis=1).astype(jnp.bfloat16)


def sum_taps(taps):
    return pl.pallas_call(
        sum_kernel,
        out_shape=jax.ShapeDtypeStruct((3, 3, 32, 128), jnp.bfloat16),
        in_specs=[pl.BlockSpec(memory_space=pltpu.VMEM)],
        out_specs=pl.BlockSpec(memory_space=pltpu.VMEM),
        compiler_params=pltpu.CompilerParams(vmem_limit_bytes=4 * 1024 * 1024),
        name="sum_taps",
    )(taps)


def spread_kernel(kernel):
    both = sum_taps(jnp.swapaxes(kernel, 3, 4))
    split = both.reshape(3, 3, 2, 2, 2, 2, 2, 128)
    moved = jnp.transpose(split, (2, 5, 3, 0, 1, 6, 4, 7))
    flat = moved.reshape(2, 2, 1, 2, 3, 3, 2, 2, 128)
    return jnp.broadcast_to(flat, (2, 2, 2, 2, 3, 3, 2, 2, 128))


def own_chunk(kernel):
    pieces = spread_kernel(kernel).reshape(16, 3, 3, 2, 2, 128)
    got = lax.all_to_all(pieces, ("x0", "zh", "zl1", "zl0"), 0, 0, tiled=True)
    got = got.reshape(4, 4, 3, 3, 2, 2, 128)
    return jnp.transpose(got, (3, 4, 1, 5, 2, 0, 6)).reshape(3, 16, 1536)


def own_rows(latent):
    rows = jnp.transpose(latent, (1, 0, 2, 3))
    tile = ("y", "zl1", "zl0", "k")
    up = [(i, i + 1) for i in range(63)]
    above = lax.ppermute(rows[3:], tile, up)
    below = lax.ppermute(rows[:1], tile, [(b, a) for a, b in up])
    return jnp.concatenate([above, rows, below], axis=0)


def start_copy(copies, sems, src, dst):
    copy = pltpu.make_async_copy(src, dst, sems.at[len(copies)])
    copy.start()
    copies.append(copy)


def pack_kernel(at_ref, here, over_x, over_z, over_both, x_ref, sems):
    x0, zh, zl0 = (at_ref[n] for n in range(3))
    copies = []
    for rows, x, z in ((here, x0, zl0), (over_x, 1 - x0, zl0), (over_z, x0, 1 - zl0), (over_both, 1 - x0, 1 - zl0)):
        for n, h in enumerate((zh, 1 - zh)):
            start_copy(copies, sems, rows.at[n], x_ref.at[z, :, :, 2 * x + h])
    for copy in copies:
        copy.wait()


def pack(at, rows):
    return pl.pallas_call(
        pack_kernel,
        out_shape=jax.ShapeDtypeStruct((2, 6, 2, 4, 64, 128), jnp.bfloat16),
        in_specs=[pl.BlockSpec(memory_space=pltpu.SMEM)] + [pl.BlockSpec(memory_space=pl.ANY)] * 4,
        out_specs=pl.BlockSpec(memory_space=pltpu.VMEM),
        scratch_shapes=[pltpu.SemaphoreType.DMA((8,))],
        compiler_params=pltpu.CompilerParams(vmem_limit_bytes=4 * 1024 * 1024),
        cost_estimate=pl.CostEstimate(flops=0, bytes_accessed=3_200_000, transcendentals=0),
        name="pack",
    )(at, *rows)


def conv_kernel(at_ref, x_ref, mine, other, bias_ref, perm_ref, out_ref, even_ref, odd_ref):
    first = at_ref[3] == 0
    lane = lax.broadcasted_iota(jnp.int32, (256, 128), 1)
    count = 8 // ROWS

    def place(n):
        part = lax.rem(n, count)
        return part * ROWS // 4, lax.rem(part * ROWS, 4), n // count

    def product(n):
        z, row, frame = place(n)
        sides = []
        for q in range(ROWS):
            parts = []
            for b in range(3):
                for chan in range(4):
                    parts.append(x_ref[z, row + q + b, 0, chan])
                    parts.append(x_ref[z, row + q + b, frame, chan])
            sides.append(jnp.concatenate(parts, axis=0))
        taps = [half[y, c] for c in range(3) for y in range(NY) for half in (mine, other)]
        taps = jnp.concatenate(taps, axis=0)
        return jnp.dot(taps, jnp.concatenate(sides, axis=1), preferred_element_type=jnp.float32)

    def finish(total_ref, n):
        z, row, frame = place(n)
        mixed = []
        for q in range(ROWS):
            lanes = pl.ds(q * 128, 128)
            before = jnp.where(lane == 0, 0.0, pltpu.roll(total_ref[:256, lanes], 1, 1))
            after = jnp.where(lane == 127, 0.0, pltpu.roll(total_ref[512:, lanes], 127, 1))
            conv = before + total_ref[256:512, lanes] + after + bias_ref[...]
            conv = conv.reshape(NY, 2, 2, 8, 128)
            conv = jnp.where(first, conv, jnp.concatenate([conv[:, 1:], conv[:, :1]], axis=1))
            mixed.append(jnp.concatenate([conv[:, :, s].reshape(128, 128) for s in range(2)], axis=1))
        mixed = jnp.concatenate(mixed, axis=0).astype(jnp.bfloat16)
        mixed = jnp.dot(mixed, perm_ref[...], preferred_element_type=jnp.float32).astype(jnp.bfloat16)
        for q in range(ROWS):
            out_ref[4 * z + row + q, frame] = mixed[128 * q : 128 * q + 128]

    def step(i, carry):
        n = 2 * i
        first = product(n)
        finish(odd_ref, jnp.maximum(n - 1, 0))
        even_ref[...] = first
        second = product(n + 1)
        finish(even_ref, n)
        odd_ref[...] = second
        return carry

    lax.fori_loop(0, count, step, 0)
    finish(odd_ref, 2 * count - 1)


def convolve(at, rows, chunks, bias, perm):
    return pl.pallas_call(
        conv_kernel,
        out_shape=jax.ShapeDtypeStruct((8, 2, 128, 256), jnp.bfloat16),
        in_specs=[pl.BlockSpec(memory_space=pltpu.SMEM)]
        + [pl.BlockSpec(memory_space=pltpu.VMEM)] * 5,
        out_specs=pl.BlockSpec(memory_space=pltpu.VMEM),
        scratch_shapes=[
            pltpu.VMEM((768, 128 * ROWS), jnp.float32),
            pltpu.VMEM((768, 128 * ROWS), jnp.float32),
        ],
        compiler_params=pltpu.CompilerParams(vmem_limit_bytes=18 * 1024 * 1024),
        cost_estimate=pl.CostEstimate(flops=4_900_000_000, bytes_accessed=6_000_000, transcendentals=0),
        name="conv",
    )(at, rows, *chunks, bias, perm)


def local(latent, kernel, bias):
    x1, x0, zh, zl0, core = (lax.axis_index(a) for a in ("x1", "x0", "zh", "zl0", "k"))
    picked = bias.reshape(NY, 4, 2, 2, 2, 2, 2, 2)[:, :, :, x0, zl0, :, zh, :]
    picked = jnp.where(core == 0, picked, picked[:, :, ::-1])
    column = jnp.transpose(picked, (0, 2, 4, 1, 3)).reshape(256, 1)
    column = jnp.broadcast_to(jnp.where(x1 == 0, column, 0.0), (256, 128))
    rows = own_rows(latent)
    own = own_chunk(kernel)
    own, rows, column = lax.optimization_barrier((own, rows, column))

    mine = lax.all_to_all(jnp.broadcast_to(own, (NY, *own.shape)), "y", 0, 0, tiled=True)
    rows = jnp.stack([rows, swap(rows, "zh")])
    over_x, over_z = swap(rows, "x0"), swap(rows, "zl0")
    over_both = lax.ppermute(rows, ("x0", "zl0"), [(i, 3 - i) for i in range(4)])
    mine, rows, over_x, over_z, over_both = lax.optimization_barrier((mine, rows, over_x, over_z, over_both))
    at = jnp.stack([x0, zh, zl0, core]).astype(jnp.int32)
    packed = pack(at, (rows, over_x, over_z, over_both))
    other = swap(mine, "k")

    place = jnp.arange(256)
    perm = ((2 * (place % 128) + place // 128)[:, None] == place[None, :]).astype(jnp.bfloat16)
    out = convolve(at, packed, (mine, other), column, perm)
    got = lax.all_to_all(out, ("zl0", "x1", "x0"), 0, 0, tiled=True).reshape(2, 2, 2, 2, 128, 256)
    total = (got[:, 0].astype(jnp.float32) + got[:, 1].astype(jnp.float32)).astype(jnp.bfloat16)
    total = total.reshape(2, 2, 2, NY, 2, 4, 2, 256)
    return jnp.transpose(total, (2, 3, 5, 4, 1, 0, 6, 7)).reshape(2, 1, 512, 256)


def solution(mesh):
    fine = Mesh(mesh.devices.reshape(SIZES), AXES)
    tile = ("y", "zl1", "zl0", "k")
    chan = ("x1", "x0", "zh")
    return jax.shard_map(
        local,
        mesh=fine,
        in_specs=(P(None, tile, chan, None), P(None, None, None, chan, tile), P()),
        out_specs=P(None, tile + chan, None, None),
        check_vma=False,
    )
```

```python
import jax
import jax.numpy as jnp
from jax import lax
from jax.experimental import pallas as pl
from jax.experimental.pallas import tpu as pltpu
from jax.sharding import Mesh, PartitionSpec as P

AXES = ("x1", "x0", "zh", "y", "zl1", "zl0", "k")
SIZES = (2, 2, 2, 8, 2, 2, 2)
NY = 8
ROWS = 4


def ring(size, step):
    return [(i, (i + step) % size) for i in range(size)]


def swap(array, axis):
    return lax.ppermute(array, axis, ring(2, 1))


def sum_kernel(taps_ref, out_ref):
    for b in range(3):
        for c in range(3):
            k01 = taps_ref[0, b, c].astype(jnp.float32) + taps_ref[1, b, c].astype(jnp.float32)
            k2 = taps_ref[2, b, c].astype(jnp.float32)
            out_ref[b, c] = jnp.concatenate([k01, k2], axis=1).astype(jnp.bfloat16)


def sum_taps(taps):
    return pl.pallas_call(
        sum_kernel,
        out_shape=jax.ShapeDtypeStruct((3, 3, 32, 128), jnp.bfloat16),
        in_specs=[pl.BlockSpec(memory_space=pltpu.VMEM)],
        out_specs=pl.BlockSpec(memory_space=pltpu.VMEM),
        compiler_params=pltpu.CompilerParams(vmem_limit_bytes=4 * 1024 * 1024),
        name="sum_taps",
    )(taps)


def spread_kernel(kernel):
    both = sum_taps(jnp.swapaxes(kernel, 3, 4))
    split = both.reshape(3, 3, 2, 2, 2, 2, 2, 128)
    moved = jnp.transpose(split, (2, 5, 3, 0, 1, 6, 4, 7))
    flat = moved.reshape(2, 2, 1, 2, 3, 3, 2, 2, 128)
    return jnp.broadcast_to(flat, (2, 2, 2, 2, 3, 3, 2, 2, 128))


def own_chunk(kernel):
    pieces = spread_kernel(kernel).reshape(16, 3, 3, 2, 2, 128)
    got = lax.all_to_all(pieces, ("x0", "zh", "zl1", "zl0"), 0, 0, tiled=True)
    got = got.reshape(4, 4, 3, 3, 2, 2, 128)
    return jnp.transpose(got, (3, 4, 1, 5, 2, 0, 6)).reshape(3, 16, 1536)


def own_rows(latent):
    rows = jnp.transpose(latent, (1, 0, 2, 3))
    tile = ("y", "zl1", "zl0", "k")
    up = [(i, i + 1) for i in range(63)]
    above = lax.ppermute(rows[3:], tile, up)
    below = lax.ppermute(rows[:1], tile, [(b, a) for a, b in up])
    return jnp.concatenate([above, rows, below], axis=0)


def start_copy(copies, sems, src, dst):
    copy = pltpu.make_async_copy(src, dst, sems.at[len(copies)])
    copy.start()
    copies.append(copy)


def pack_kernel(at_ref, here, over_x, over_z, over_both, x_ref, sems):
    x0, zh, zl0 = (at_ref[n] for n in range(3))
    copies = []
    for rows, x, z in ((here, x0, zl0), (over_x, 1 - x0, zl0), (over_z, x0, 1 - zl0), (over_both, 1 - x0, 1 - zl0)):
        for n, h in enumerate((zh, 1 - zh)):
            start_copy(copies, sems, rows.at[n], x_ref.at[z, :, :, 2 * x + h])
    for copy in copies:
        copy.wait()


def pack(at, rows):
    return pl.pallas_call(
        pack_kernel,
        out_shape=jax.ShapeDtypeStruct((2, 6, 2, 4, 64, 128), jnp.bfloat16),
        in_specs=[pl.BlockSpec(memory_space=pltpu.SMEM)] + [pl.BlockSpec(memory_space=pl.ANY)] * 4,
        out_specs=pl.BlockSpec(memory_space=pltpu.VMEM),
        scratch_shapes=[pltpu.SemaphoreType.DMA((8,))],
        compiler_params=pltpu.CompilerParams(vmem_limit_bytes=4 * 1024 * 1024),
        cost_estimate=pl.CostEstimate(flops=0, bytes_accessed=3_200_000, transcendentals=0),
        name="pack",
    )(at, *rows)


def conv_kernel(at_ref, x_ref, mine, other, bias_ref, perm_ref, out_ref, even_ref, odd_ref):
    first = at_ref[3] == 0
    lane = lax.broadcasted_iota(jnp.int32, (256, 128), 1)
    count = 8 // ROWS

    def place(n):
        part = lax.rem(n, count)
        return part * ROWS // 4, lax.rem(part * ROWS, 4), n // count

    def product(n):
        z, row, frame = place(n)
        sides = []
        for q in range(ROWS):
            parts = []
            for b in range(3):
                for chan in range(4):
                    parts.append(x_ref[z, row + q + b, 0, chan])
                    parts.append(x_ref[z, row + q + b, frame, chan])
            sides.append(jnp.concatenate(parts, axis=0))
        taps = [half[y, c] for c in range(3) for y in range(NY) for half in (mine, other)]
        taps = jnp.concatenate(taps, axis=0)
        return jnp.dot(taps, jnp.concatenate(sides, axis=1), preferred_element_type=jnp.float32)

    def finish(total_ref, n):
        z, row, frame = place(n)
        mixed = []
        for q in range(ROWS):
            lanes = pl.ds(q * 128, 128)
            before = jnp.where(lane == 0, 0.0, pltpu.roll(total_ref[:256, lanes], 1, 1))
            after = jnp.where(lane == 127, 0.0, pltpu.roll(total_ref[512:, lanes], 127, 1))
            conv = before + total_ref[256:512, lanes] + after + bias_ref[...]
            conv = conv.reshape(NY, 2, 2, 8, 128)
            conv = jnp.where(first, conv, jnp.concatenate([conv[:, 1:], conv[:, :1]], axis=1))
            mixed.append(jnp.concatenate([conv[:, :, s].reshape(128, 128) for s in range(2)], axis=1))
        mixed = jnp.concatenate(mixed, axis=0).astype(jnp.bfloat16)
        mixed = jnp.dot(mixed, perm_ref[...], preferred_element_type=jnp.float32).astype(jnp.bfloat16)
        for q in range(ROWS):
            out_ref[2 * (row + q) + z, frame] = mixed[128 * q : 128 * q + 128]

    def step(i, carry):
        n = 2 * i
        first = product(n)
        finish(odd_ref, jnp.maximum(n - 1, 0))
        even_ref[...] = first
        second = product(n + 1)
        finish(even_ref, n)
        odd_ref[...] = second
        return carry

    lax.fori_loop(0, count, step, 0)
    finish(odd_ref, 2 * count - 1)


def convolve(at, rows, chunks, bias, perm):
    return pl.pallas_call(
        conv_kernel,
        out_shape=jax.ShapeDtypeStruct((8, 2, 128, 256), jnp.bfloat16),
        in_specs=[pl.BlockSpec(memory_space=pltpu.SMEM)]
        + [pl.BlockSpec(memory_space=pltpu.VMEM)] * 5,
        out_specs=pl.BlockSpec(memory_space=pltpu.VMEM),
        scratch_shapes=[
            pltpu.VMEM((768, 128 * ROWS), jnp.float32),
            pltpu.VMEM((768, 128 * ROWS), jnp.float32),
        ],
        compiler_params=pltpu.CompilerParams(vmem_limit_bytes=18 * 1024 * 1024),
        cost_estimate=pl.CostEstimate(flops=4_900_000_000, bytes_accessed=6_000_000, transcendentals=0),
        name="conv",
    )(at, rows, *chunks, bias, perm)


def local(latent, kernel, bias):
    x1, x0, zh, zl0, core = (lax.axis_index(a) for a in ("x1", "x0", "zh", "zl0", "k"))
    picked = bias.reshape(NY, 4, 2, 2, 2, 2, 2, 2)[:, :, :, x0, zl0, :, zh, :]
    picked = jnp.where(core == 0, picked, picked[:, :, ::-1])
    column = jnp.transpose(picked, (0, 2, 4, 1, 3)).reshape(256, 1)
    column = jnp.broadcast_to(jnp.where(x1 == 0, column, 0.0), (256, 128))
    rows = own_rows(latent)
    own = own_chunk(kernel)
    own, rows, column = lax.optimization_barrier((own, rows, column))

    mine = lax.all_to_all(jnp.broadcast_to(own, (NY, *own.shape)), "y", 0, 0, tiled=True)
    rows = jnp.stack([rows, swap(rows, "zh")])
    over_x, over_z = swap(rows, "x0"), swap(rows, "zl0")
    over_both = lax.ppermute(rows, ("x0", "zl0"), [(i, 3 - i) for i in range(4)])
    mine, rows, over_x, over_z, over_both = lax.optimization_barrier((mine, rows, over_x, over_z, over_both))
    at = jnp.stack([x0, zh, zl0, core]).astype(jnp.int32)
    packed = pack(at, (rows, over_x, over_z, over_both))
    other = swap(mine, "k")

    place = jnp.arange(256)
    perm = ((2 * (place % 128) + place // 128)[:, None] == place[None, :]).astype(jnp.bfloat16)
    out = convolve(at, packed, (mine, other), column, perm)
    got = lax.all_to_all(out, ("x1", "x0", "zl0"), 0, 0, tiled=True).reshape(2, 2, 2, 2, 128, 256)
    total = (got[0].astype(jnp.float32) + got[1].astype(jnp.float32)).astype(jnp.bfloat16)
    total = total.reshape(2, 2, 2, NY, 2, 4, 2, 256)
    return jnp.transpose(total, (2, 3, 5, 4, 0, 1, 6, 7)).reshape(2, 1, 512, 256)


def solution(mesh):
    fine = Mesh(mesh.devices.reshape(SIZES), AXES)
    tile = ("y", "zl1", "zl0", "k")
    chan = ("x1", "x0", "zh")
    return jax.shard_map(
        local,
        mesh=fine,
        in_specs=(P(None, tile, chan, None), P(None, None, None, chan, tile), P()),
        out_specs=P(None, tile + chan, None, None),
        check_vma=False,
    )
```
